256 devices in a mesh: layer: 4 (over z_hi, core), tile: 64 (over x, z_lo, y).
Axes of the slice: x: 4, y: 4, z: 8 (z_hi: 2, z_lo: 4; z = z_hi * 4 + z_lo), core: 2. Of those that a mesh axis runs over, the one named last changes fastest.
Arguments:
- sources: bfloat16 [4, 2, 64, 32768], P('layer', None, None, 'tile'), may hold values from -6 to 6
- down_blocks: bfloat16 [4, 3, 2, 32768, 512], P('layer', None, None, 'tile'), may hold values from -0.109375 to 0.109375
- up_blocks: bfloat16 [4, 3, 2, 32768, 512], P('layer', None, None, 'tile'), may hold values from -0.109375 to 0.109375
Outputs:
- down_trace: bfloat16 [4, 2, 64, 32768], P('layer', None, None, 'tile')
- up_trace: bfloat16 [4, 2, 64, 32768], P('layer', None, None, 'tile')
The draws below stay inside these ranges and needn't reach their ends.
All inputs are finite; a program needn't handle non-finite values.
Results may differ from the reference program's by a relative error of at most 0.011.
Values may be sent and summed in bfloat16 or wider, within the bound.
No kernel may reach another device: no remote copies, remote signals or barrier semaphores. Data moves between devices by JAX's collectives and lax.ppermute only.
A program may use at most 128 MiB of HBM per device.

```python
import jax
import jax.numpy as jnp
from jax import lax

CT = 512
SRC = 64
LAYERS = 4
CELLS = 32768
N_TILE = 64


def level_of(key, dims, shards, low, top_value):
    gain = 1.0
    for position, blocks in shards:
        draws = jax.random.uniform(jax.random.fold_in(jax.random.fold_in(key, 6), position), (blocks,), jnp.float32, low / len(shards), top_value / len(shards))
        gain = gain * jnp.repeat(jnp.exp(draws), dims[position] // blocks).reshape((-1,) + (1,) * (len(dims) - 1 - position))
    return gain


def noise(key, extent, width, bound, shards=(), dtype=jnp.bfloat16):
    drawn = width * jax.random.normal(key, extent, jnp.float32)
    if shards:
        drawn = drawn * level_of(key, extent, shards, -0.22, 0.18)
    return jnp.clip(drawn, -bound, bound).astype(dtype)


def setup_inputs(seed: int = 0) -> dict:
    key_of = jax.random.split(jax.random.key(seed), 4)
    return {
        "sources": noise(key_of[0], (LAYERS, 2, SRC, CELLS), 1.0, 6.0, ((0, 4), (3, 64))),
        "down_blocks": noise(key_of[1], (LAYERS, 3, 2, CELLS, CT), (6 * CT) ** -0.5, 0.109375, ((0, 4), (3, 64))),
        "up_blocks": noise(key_of[2], (LAYERS, 3, 2, CELLS, CT), (6 * CT) ** -0.5, 0.109375, ((0, 4), (3, 64))),
    }


def couple_tiles(trace, blocks):
    tile_count = N_TILE
    tile_cells = CT
    shaped = trace.astype(jnp.float32).reshape(2, trace.shape[1], tile_count, tile_cells)
    zeros_rim = jnp.zeros((2, trace.shape[1], 1, tile_cells), jnp.float32)
    lower_tile = jnp.concatenate([zeros_rim, shaped[:, :, :-1]], axis=2)
    upper_tile = jnp.concatenate([shaped[:, :, 1:], zeros_rim], axis=2)
    matrices = blocks.reshape(3, 2, tile_count, tile_cells, tile_cells)
    real_part = jnp.zeros(shaped.shape[1:], jnp.float32)
    imag_part = jnp.zeros(shaped.shape[1:], jnp.float32)
    for number, neighbour in enumerate((shaped, lower_tile, upper_tile)):
        block_real = matrices[number, 0].astype(jnp.float32)
        block_imag = matrices[number, 1].astype(jnp.float32)
        high = lax.Precision.HIGHEST
        real_part = real_part + jnp.einsum("stc,tcd->std", neighbour[0], block_real, precision=high) - jnp.einsum("stc,tcd->std", neighbour[1], block_imag, precision=high)
        imag_part = imag_part + jnp.einsum("stc,tcd->std", neighbour[0], block_imag, precision=high) + jnp.einsum("stc,tcd->std", neighbour[1], block_real, precision=high)
    return jnp.stack([real_part, imag_part]).reshape(2, trace.shape[1], tile_count * tile_cells)


def reference(sources, down_blocks, up_blocks):
    layer_count = sources.shape[0]
    previous = jnp.zeros(sources.shape[1:], jnp.bfloat16)
    downward = []
    for layer_number in range(layer_count):
        previous = (couple_tiles(previous, down_blocks[layer_number]) + sources[layer_number].astype(jnp.float32)).astype(jnp.bfloat16)
        downward.append(previous)
    previous = jnp.zeros(sources.shape[1:], jnp.bfloat16)
    upward = [None] * layer_count
    for layer_number in range(layer_count - 1, -1, -1):
        previous = (couple_tiles(previous, up_blocks[layer_number]) + downward[layer_number].astype(jnp.float32)).astype(jnp.bfloat16)
        upward[layer_number] = previous
    return jnp.stack(downward), jnp.stack(upward)
```

```python
import functools

import jax
import jax.numpy as jnp
from jax import lax
from jax.experimental import pallas as pl
from jax.experimental.pallas import tpu as pltpu
from jax.sharding import PartitionSpec as P

AXES = ("layer", "tile")
VMEM_LIMIT = 32 * 1024 * 1024


def far_mate(tile, tiles):
    return (tile + 1) % tiles if tile % 2 else (tile - 1) % tiles


def near_mate(tile, tiles):
    return tile - 1 if tile % 2 else tile + 1


def same(tile, tiles):
    return tile


def hop_pairs(route, mate, tiles):
    pairs = []
    for number, (source, target) in enumerate(route):
        for tile in range(tiles):
            there = mate(tile, tiles) if number == 0 else tile
            pairs.append((source * tiles + tile, target * tiles + there))
    return pairs


def step_kernel(own_ref, near_ref, far_ref, blocks_ref, addend_ref, out_ref):
    tiles = lax.axis_size("tile")
    tile = lax.axis_index("tile")
    odd = lax.rem(tile, 2)
    rows, cells = own_ref.shape[1:]
    edge = jnp.logical_or(tile == 0, tile == tiles - 1)

    def product(values, number):
        by_real = jnp.dot(values, blocks_ref[number, 0], preferred_element_type=jnp.float32)
        by_imag = jnp.dot(values, blocks_ref[number, 1], preferred_element_type=jnp.float32)
        return by_real, by_imag

    def stacked(ref):
        return ref[...].reshape(2 * rows, cells)

    far = stacked(far_ref)
    far = jnp.where(edge, jnp.zeros_like(far), far)
    own_real, own_imag = product(stacked(own_ref), 0)
    near_real, near_imag = product(stacked(near_ref), 2 - odd)
    far_real, far_imag = product(far, 1 + odd)
    by_real = own_real + near_real + far_real
    by_imag = own_imag + near_imag + far_imag
    out_ref[0] = (by_real[:rows] - by_imag[rows:] + addend_ref[0].astype(jnp.float32)).astype(out_ref.dtype)
    out_ref[1] = (by_imag[:rows] + by_real[rows:] + addend_ref[1].astype(jnp.float32)).astype(out_ref.dtype)


def step(own, near, far, blocks, addend):
    vmem = pl.BlockSpec(memory_space=pltpu.VMEM)
    return pl.pallas_call(
        step_kernel,
        out_shape=jax.ShapeDtypeStruct(own.shape, own.dtype),
        in_specs=[vmem] * 5,
        out_specs=vmem,
        compiler_params=pltpu.CompilerParams(vmem_limit_bytes=VMEM_LIMIT),
        cost_estimate=pl.CostEstimate(
            flops=24 * own.shape[1] * own.shape[2] * own.shape[2],
            bytes_accessed=blocks.size * 2 + own.size * 10,
            transcendentals=0,
        ),
    )(own, near, far, blocks, addend)


ROUTES = {
    (0, 1): ((0, 1), (1, 0), (2, 3), (3, 2)),
    (1, 0): ((1, 0), (0, 1), (2, 3), (3, 2)),
    (1, 2): ((1, 2), (2, 3), (3, 0), (0, 1)),
    (2, 1): ((2, 1), (1, 0), (0, 3), (3, 2)),
    (2, 3): ((2, 3), (3, 2), (0, 1), (1, 0)),
    (3, 2): ((3, 2), (2, 3), (0, 1), (1, 0)),
}


def hop(values, source, target, blocks, addend):
    tiles = lax.axis_size("tile")
    route = ROUTES[source, target]
    far = lax.ppermute(values, AXES, hop_pairs(route, far_mate, tiles))
    near = lax.ppermute(values, AXES, hop_pairs(route, near_mate, tiles))
    own = lax.ppermute(values, AXES, hop_pairs(route, same, tiles))
    return step(own, near, far, blocks, addend)


def per_device(sources, down_blocks, up_blocks):
    layer = lax.axis_index("layer")
    source = sources[0]
    down = pltpu.with_memory_space_constraint(down_blocks[0], pltpu.VMEM)
    up = pltpu.with_memory_space_constraint(up_blocks[0], pltpu.VMEM)
    values = source
    falling = source
    for index in range(1, 4):
        values = hop(values, index - 1, index, down, source)
        falling = jnp.where(layer == index, values, falling)
    rising = falling
    for index in (2, 1, 0):
        values = hop(values, index + 1, index, up, falling)
        rising = jnp.where(layer == index, values, rising)
    return (falling[None], rising[None])


def solution(mesh):
    return jax.shard_map(
        per_device,
        mesh=mesh,
        in_specs=(
            P("layer", None, None, "tile"),
            P("layer", None, None, "tile", None),
            P("layer", None, None, "tile", None),
        ),
        out_specs=(P("layer", None, None, "tile"), P("layer", None, None, "tile")),
        check_vma=False,
    )
```

```python
import functools

import jax
import jax.numpy as jnp
from jax import lax
from jax.experimental import pallas as pl
from jax.experimental.pallas import tpu as pltpu
from jax.sharding import PartitionSpec as P

AXES = ("layer", "tile")
VMEM_LIMIT = 16 * 1024 * 1024


def far_mate(tile, tiles):
    mate = tile + 1 if tile % 2 else tile - 1
    return mate if 0 <= mate < tiles else tile


def near_mate(tile, tiles):
    return tile - 1 if tile % 2 else tile + 1


def same(tile, tiles):
    return tile


def mirror(tile, tiles):
    x, z, y = tile // 16, tile // 4 % 4, tile % 4
    return 16 * x + 4 * (3 - z) + y


def pairs_of(route, tiles):
    return [
        (source * tiles + tile, target * tiles + mate(tile, tiles))
        for source, target, mate in route
        for tile in range(tiles)
    ]


def within_chip(source, target, mate):
    one, two = [layer for layer in range(4) if layer not in (source, target)]
    return ((source, target, mate), (target, source, same), (one, two, same), (two, one, same))


def across(source, target, mate):
    beyond = 3 if target == 2 else 0
    behind = 3 - beyond
    return ((source, target, mate), (target, beyond, same), (beyond, behind, mirror), (behind, source, same))


def beside(source, target):
    beyond = 3 if target == 2 else 0
    behind = 3 - beyond
    return ((target, target, near_mate), (beyond, beyond, near_mate), (source, behind, same), (behind, source, same))


def permute(values, route):
    return lax.ppermute(values, AXES, pairs_of(route, lax.axis_size("tile")))


def load_kernel(layer, blocks_ref, after_ref, held_ref, sems):
    @pl.when(lax.axis_index("layer") == layer)
    def _():
        count, parts = blocks_ref.shape[:2]
        copies = [
            pltpu.make_async_copy(blocks_ref.at[i, j], held_ref.at[i, j], sems.at[i, j])
            for i in range(count)
            for j in range(parts)
        ]
        for copy in copies:
            copy.start()
        for copy in copies:
            copy.wait()


def load(blocks, after, layer):
    return pl.pallas_call(
        functools.partial(load_kernel, layer),
        out_shape=pltpu.VMEM(blocks.shape, blocks.dtype),
        in_specs=[pl.BlockSpec(memory_space=pl.ANY)] * 2,
        out_specs=pl.BlockSpec(memory_space=pltpu.VMEM),
        scratch_shapes=[pltpu.SemaphoreType.DMA(blocks.shape[:2])],
        compiler_params=pltpu.CompilerParams(vmem_limit_bytes=VMEM_LIMIT),
        cost_estimate=pl.CostEstimate(flops=0, bytes_accessed=blocks.size * 4, transcendentals=0),
    )(pltpu.with_memory_space_constraint(blocks, pltpu.HBM), after)


def step_kernel(layer, far_ref, near_ref, own_ref, blocks_ref, addend_ref, *rest):
    *kept_ref, out_ref = rest
    tiles = lax.axis_size("tile")
    tile = lax.axis_index("tile")
    odd = lax.rem(tile, 2)
    rows, cells = own_ref.shape[1:]
    edge = jnp.logical_or(tile == 0, tile == tiles - 1)
    here = lax.axis_index("layer") == layer

    def stacked(ref):
        return ref[...].reshape(2 * rows, cells)

    def product(values, number):
        by_real = jnp.dot(values, blocks_ref[number, 0], preferred_element_type=jnp.float32)
        by_imag = jnp.dot(values, blocks_ref[number, 1], preferred_element_type=jnp.float32)
        return by_real, by_imag

    far = stacked(far_ref)
    far = jnp.where(edge, jnp.zeros_like(far), far)
    own_real, own_imag = product(stacked(own_ref), 0)
    near_real, near_imag = product(stacked(near_ref), 2 - odd)
    far_real, far_imag = product(far, 1 + odd)
    by_real = own_real + near_real + far_real
    by_imag = own_imag + near_imag + far_imag
    real = (by_real[:rows] - by_imag[rows:] + addend_ref[0].astype(jnp.float32)).astype(out_ref.dtype)
    imag = (by_imag[:rows] + by_real[rows:] + addend_ref[1].astype(jnp.float32)).astype(out_ref.dtype)
    if kept_ref:
        real = jnp.where(here, real, kept_ref[0][0])
        imag = jnp.where(here, imag, kept_ref[0][1])
    out_ref[0] = real
    out_ref[1] = imag


def step(layer, own, near, far, blocks, addend, *kept):
    vmem = pl.BlockSpec(memory_space=pltpu.VMEM)
    return pl.pallas_call(
        functools.partial(step_kernel, layer),
        out_shape=jax.ShapeDtypeStruct(own.shape, own.dtype),
        in_specs=[vmem] * (5 + len(kept)),
        out_specs=vmem,
        compiler_params=pltpu.CompilerParams(vmem_limit_bytes=VMEM_LIMIT),
        cost_estimate=pl.CostEstimate(
            flops=24 * own.shape[1] * own.shape[2] * own.shape[2],
            bytes_accessed=blocks.size * 2 + own.size * 10,
            transcendentals=0,
        ),
    )(far, near, own, blocks, addend, *kept)


def hop(values, source, target, blocks, addend, *kept):
    if source + target == 3:
        own = permute(values, across(source, target, same))
        far = permute(values, across(source, target, far_mate))
        near = permute(own, beside(source, target))
    else:
        far = permute(values, within_chip(source, target, far_mate))
        near = permute(values, within_chip(source, target, near_mate))
        own = permute(values, within_chip(source, target, same))
    held = load(blocks, values, target)
    return step(target, own, near, far, held, addend, *kept)


def per_device(sources, down_blocks, up_blocks):
    layer = lax.axis_index("layer")
    source = sources[0]
    values = falling = source
    for index in (1, 2, 3):
        values = hop(values, index - 1, index, down_blocks[0], source)
        falling = jnp.where(layer == index, values, falling)
    rising = falling
    for index in (2, 1):
        values = hop(values, index + 1, index, up_blocks[0], falling)
        rising = jnp.where(layer == index, values, rising)
    rising = hop(values, 1, 0, up_blocks[0], falling, rising)
    return (falling[None], rising[None])


def solution(mesh):
    return jax.shard_map(
        per_device,
        mesh=mesh,
        in_specs=(
            P("layer", None, None, "tile"),
            P("layer", None, None, "tile", None),
            P("layer", None, None, "tile", None),
        ),
        out_specs=(P("layer", None, None, "tile"), P("layer", None, None, "tile")),
        check_vma=False,
    )
```

```python
import functools

import jax
import jax.numpy as jnp
from jax import lax
from jax.experimental import pallas as pl
from jax.experimental.pallas import tpu as pltpu
from jax.sharding import PartitionSpec as P

AXES = ("layer", "tile")
VMEM_LIMIT = 16 * 1024 * 1024
FAR_FIRST = ("far", "near", "own")
ORDERS = (FAR_FIRST, FAR_FIRST, ("near", "own", "far"), FAR_FIRST, FAR_FIRST, FAR_FIRST)


def far_mate(tile, tiles):
    mate = tile + 1 if tile % 2 else tile - 1
    return mate if 0 <= mate < tiles else tile


def near_mate(tile, tiles):
    return tile - 1 if tile % 2 else tile + 1


def same(tile, tiles):
    return tile


def mirror(tile, tiles):
    x, z, y = tile // 16, tile // 4 % 4, tile % 4
    return 16 * x + 4 * (3 - z) + y


def at_seam(tile, tiles):
    return tile // 16 != far_mate(tile, tiles) // 16


def pairs_of(route, tiles, select=lambda tile, tiles: True):
    return [
        (source * tiles + tile, target * tiles + mate(tile, tiles))
        for source, target, mate in route
        for tile in range(tiles)
        if select(tile, tiles)
    ]


def within_chip(source, target, mate):
    one, two = [layer for layer in range(4) if layer not in (source, target)]
    return ((source, target, mate), (target, source, same), (one, two, same), (two, one, same))


def across(source, target):
    return (
        (source, target, same),
        (target, target ^ 1, same),
        (target ^ 1, source ^ 1, mirror),
        (source ^ 1, source, same),
    )


ON_CHIP = ((0, 1, same), (1, 0, same), (2, 3, same), (3, 2, same))


def inner_mate(tile, tiles):
    return tile if at_seam(tile, tiles) else far_mate(tile, tiles)


def over_seam(source, target, tiles):
    route = (
        (source, target, far_mate),
        (target, target ^ 1, same),
        (target ^ 1, source ^ 1, far_mate),
        (source ^ 1, source, same),
    )
    return pairs_of(route, tiles, at_seam) + pairs_of(ON_CHIP, tiles, lambda *tile: not at_seam(*tile))


def permute(values, pairs):
    return lax.ppermute(values, AXES, pairs)


def load_kernel(layers, blocks_ref, after_ref, held_ref, sems):
    here = lax.axis_index("layer")

    @pl.when(functools.reduce(jnp.logical_or, [here == layer for layer in layers]))
    def _():
        count, parts = blocks_ref.shape[:2]
        copies = [
            pltpu.make_async_copy(blocks_ref.at[i, j], held_ref.at[i, j], sems.at[i, j])
            for i in range(count)
            for j in range(parts)
        ]
        for copy in copies:
            copy.start()
        for copy in copies:
            copy.wait()


def load(blocks, after, *layers):
    return pl.pallas_call(
        functools.partial(load_kernel, layers),
        out_shape=pltpu.VMEM(blocks.shape, blocks.dtype),
        in_specs=[pl.BlockSpec(memory_space=pl.ANY)] * 2,
        out_specs=pl.BlockSpec(memory_space=pltpu.VMEM),
        scratch_shapes=[pltpu.SemaphoreType.DMA(blocks.shape[:2])],
        compiler_params=pltpu.CompilerParams(vmem_limit_bytes=VMEM_LIMIT),
        cost_estimate=pl.CostEstimate(flops=0, bytes_accessed=blocks.size * 4, transcendentals=0),
    )(pltpu.with_memory_space_constraint(blocks, pltpu.HBM), after)


def step_kernel(layer, names, *refs):
    *refs, out_ref = refs
    refs = dict(zip(names, refs))
    here = lax.axis_index("layer") == layer

    if "kept" in refs:

        @pl.when(jnp.logical_not(here))
        def _():
            out_ref[...] = refs["kept"][...]

    @pl.when(here)
    def _():
        product_and_sum(refs, out_ref)


def product_and_sum(refs, out_ref):
    own_ref, near_ref, far_ref = refs["own"], refs["near"], refs["far"]
    blocks_ref, addend_ref = refs["blocks"], refs["addend"]
    tiles = lax.axis_size("tile")
    tile = lax.axis_index("tile")
    odd = lax.rem(tile, 2)
    rows, cells = own_ref.shape[1:]
    edge = jnp.logical_or(tile == 0, tile == tiles - 1)

    def stacked(ref):
        return ref[...].reshape(2 * rows, cells)

    def product(values, number):
        by_real = jnp.dot(values, blocks_ref[number, 0], preferred_element_type=jnp.float32)
        by_imag = jnp.dot(values, blocks_ref[number, 1], preferred_element_type=jnp.float32)
        return by_real, by_imag

    far = stacked(far_ref)
    if "seam" in refs:
        place = lax.rem(tile, tiles // 4)
        far = jnp.where(jnp.logical_or(place == 0, place == tiles // 4 - 1), stacked(refs["seam"]), far)
    far = jnp.where(edge, jnp.zeros_like(far), far)
    own_real, own_imag = product(stacked(own_ref), 0)
    near_real, near_imag = product(stacked(near_ref), 2 - odd)
    far_real, far_imag = product(far, 1 + odd)
    by_real = own_real + near_real + far_real
    by_imag = own_imag + near_imag + far_imag
    real = (by_real[:rows] - by_imag[rows:] + addend_ref[0].astype(jnp.float32)).astype(out_ref.dtype)
    imag = (by_imag[:rows] + by_real[rows:] + addend_ref[1].astype(jnp.float32)).astype(out_ref.dtype)
    out_ref[0] = real
    out_ref[1] = imag


def step(layer, **operands):
    vmem = pl.BlockSpec(memory_space=pltpu.VMEM)
    addend = operands["addend"]
    return pl.pallas_call(
        functools.partial(step_kernel, layer, tuple(operands)),
        out_shape=jax.ShapeDtypeStruct(addend.shape, addend.dtype),
        in_specs=[vmem] * len(operands),
        out_specs=vmem,
        compiler_params=pltpu.CompilerParams(vmem_limit_bytes=VMEM_LIMIT),
        cost_estimate=pl.CostEstimate(
            flops=24 * addend.shape[1] * addend.shape[2] * addend.shape[2],
            bytes_accessed=operands["blocks"].size * 2 + addend.size * 10,
            transcendentals=0,
        ),
    )(*operands.values())


def spread(values, source, target, far, order):
    tiles = lax.axis_size("tile")
    mates = {"far": far, "near": near_mate, "own": same}
    return {name: permute(values, pairs_of(within_chip(source, target, mates[name]), tiles)) for name in order}


def hop(values, source, target, blocks, order, after=None, **rest):
    arrived = spread(values, source, target, far_mate, order)
    held = load(blocks, values if after is None else after, target)
    return step(target, **arrived, blocks=held, **rest)


def crossing_hop(values, source, target, blocks, order, **rest):
    tiles = lax.axis_size("tile")
    crossed = permute(values, pairs_of(across(source, target ^ 1), tiles))
    seam = permute(values, over_seam(source, target, tiles))
    arrived = spread(crossed, target ^ 1, target, inner_mate, order)
    return step(target, **arrived, seam=seam, blocks=load(blocks, values, target), **rest)


def per_device(sources, down_blocks, up_blocks):
    layer = lax.axis_index("layer")
    source, down, up = sources[0], down_blocks[0], up_blocks[0]
    down_1 = hop(source, 0, 1, down, ORDERS[0], addend=source)
    down_2 = crossing_hop(down_1, 1, 2, down, ORDERS[1], addend=source)
    down_3 = hop(down_2, 2, 3, down, ORDERS[2], addend=source)
    falling = jnp.where(layer == 0, source, jnp.where(layer == 1, down_1, jnp.where(layer == 2, down_2, down_3)))
    up_2 = hop(down_3, 3, 2, up, ORDERS[3], addend=down_2)
    up_1 = crossing_hop(up_2, 2, 1, up, ORDERS[4], addend=down_1)
    rising = jnp.where(layer == 1, up_1, jnp.where(layer == 2, up_2, down_3))
    rising = hop(up_1, 1, 0, up, ORDERS[5], down_3, addend=source, kept=rising)
    return (falling[None], rising[None])


def solution(mesh):
    return jax.shard_map(
        per_device,
        mesh=mesh,
        in_specs=(
            P("layer", None, None, "tile"),
            P("layer", None, None, "tile", None),
            P("layer", None, None, "tile", None),
        ),
        out_specs=(P("layer", None, None, "tile"), P("layer", None, None, "tile")),
        check_vma=False,
    )
```

```python
import functools

import jax
import jax.numpy as jnp
from jax import lax
from jax.experimental import pallas as pl
from jax.experimental.pallas import tpu as pltpu
from jax.sharding import PartitionSpec as P

AXES = ("layer", "tile")
VMEM_LIMIT = 16 * 1024 * 1024
FAR_FIRST = ("far", "near", "own")
ORDERS = (FAR_FIRST, FAR_FIRST, ("own", "far", "near"), FAR_FIRST, FAR_FIRST, FAR_FIRST)


def far_mate(tile, tiles):
    mate = tile + 1 if tile % 2 else tile - 1
    return mate if 0 <= mate < tiles else tile


def near_mate(tile, tiles):
    return tile - 1 if tile % 2 else tile + 1


def same(tile, tiles):
    return tile


def mirror(tile, tiles):
    x, z, y = tile // 16, tile // 4 % 4, tile % 4
    return 16 * x + 4 * (3 - z) + y


def at_seam(tile, tiles):
    return tile // 16 != far_mate(tile, tiles) // 16


def by_seam(tile, tiles):
    return at_seam(tile, tiles) or at_seam(near_mate(tile, tiles), tiles)


def inner_mate(tile, tiles):
    return tile if at_seam(tile, tiles) else far_mate(tile, tiles)


def plain_mate(tile, tiles):
    return tile if by_seam(tile, tiles) else near_mate(tile, tiles)


def over(tile, tiles):
    return (tile + 8) // 16 * 32 - 1 - tile


def pairs_of(route, tiles, select=lambda tile, tiles: True):
    return [
        (source * tiles + tile, target * tiles + mate(tile, tiles))
        for source, target, mate in route
        for tile in range(tiles)
        if select(tile, tiles)
    ]


ON_CHIP = ((0, 1, same), (1, 0, same), (2, 3, same), (3, 2, same))


def else_on_chip(route, tiles, select):
    return pairs_of(route, tiles, select) + pairs_of(ON_CHIP, tiles, lambda *tile: not select(*tile))


def within_chip(source, target, mate):
    one, two = [layer for layer in range(4) if layer not in (source, target)]
    return ((source, target, mate), (target, source, same), (one, two, same), (two, one, same))


def around(source, target, mate, back):
    return (
        (source, target, mate),
        (target, target ^ 1, same),
        (target ^ 1, source ^ 1, back),
        (source ^ 1, source, same),
    )


def across(source, target, tiles):
    return pairs_of(around(source, target, same, mirror), tiles, at_seam) + pairs_of(
        around(source, target ^ 1, same, mirror), tiles, lambda *tile: not at_seam(*tile)
    )


def permute(values, pairs):
    return lax.ppermute(values, AXES, pairs)


def load_kernel(layers, blocks_ref, after_ref, held_ref, sems):
    here = lax.axis_index("layer")

    @pl.when(functools.reduce(jnp.logical_or, [here == layer for layer in layers]))
    def _():
        count, parts = blocks_ref.shape[:2]
        copies = [
            pltpu.make_async_copy(blocks_ref.at[i, j], held_ref.at[i, j], sems.at[i, j])
            for i in range(count)
            for j in range(parts)
        ]
        for copy in copies:
            copy.start()
        for copy in copies:
            copy.wait()


def load(blocks, after, *layers):
    return pl.pallas_call(
        functools.partial(load_kernel, layers),
        out_shape=pltpu.VMEM(blocks.shape, blocks.dtype),
        in_specs=[pl.BlockSpec(memory_space=pl.ANY)] * 2,
        out_specs=pl.BlockSpec(memory_space=pltpu.VMEM),
        scratch_shapes=[pltpu.SemaphoreType.DMA(blocks.shape[:2])],
        compiler_params=pltpu.CompilerParams(vmem_limit_bytes=VMEM_LIMIT),
        cost_estimate=pl.CostEstimate(flops=0, bytes_accessed=blocks.size * 4, transcendentals=0),
    )(pltpu.with_memory_space_constraint(blocks, pltpu.HBM), after)


def seam_here(shift):
    tiles = lax.axis_size("tile")
    tile = lax.axis_index("tile")
    run = tiles // 4
    place = lax.rem(tile, run)
    outer = jnp.logical_or(tile == shift, tile == tiles - 1 - shift)
    return jnp.logical_and(jnp.logical_or(place == shift, place == run - 1 - shift), jnp.logical_not(outer))


def step_kernel(layer, names, *refs):
    *refs, out_ref = refs
    refs = dict(zip(names, refs))
    here = lax.axis_index("layer") == layer
    if "early" in refs:
        seam = seam_here(0)

        @pl.when(jnp.logical_and(here, seam))
        def _():
            out_ref[...] = refs["early"][...]

        here = jnp.logical_and(here, jnp.logical_not(seam))

    if "kept" in refs:

        @pl.when(jnp.logical_not(here))
        def _():
            out_ref[...] = refs["kept"][...]

    @pl.when(here)
    def _():
        product_and_sum(refs, out_ref)


def seam_kernel(layer, names, *refs):
    *refs, out_ref = refs

    @pl.when(jnp.logical_and(lax.axis_index("layer") == layer, seam_here(0)))
    def _():
        product_and_sum(dict(zip(names, refs)), out_ref)


def product_and_sum(refs, out_ref):
    own_ref, near_ref, far_ref = refs["own"], refs["near"], refs["far"]
    blocks_ref, addend_ref = refs["blocks"], refs["addend"]
    tiles = lax.axis_size("tile")
    tile = lax.axis_index("tile")
    odd = lax.rem(tile, 2)
    rows, cells = own_ref.shape[1:]
    edge = jnp.logical_or(tile == 0, tile == tiles - 1)

    def stacked(ref):
        return ref[...].reshape(2 * rows, cells)

    def product(values, number):
        by_real = jnp.dot(values, blocks_ref[number, 0], preferred_element_type=jnp.float32)
        by_imag = jnp.dot(values, blocks_ref[number, 1], preferred_element_type=jnp.float32)
        return by_real, by_imag

    far = stacked(far_ref)
    if "passed" in refs:
        far = jnp.where(seam_here(0), stacked(refs["passed"]), far)
    far = jnp.where(edge, jnp.zeros_like(far), far)
    near = stacked(near_ref)
    if "direct" in refs:
        near = jnp.where(seam_here(1), stacked(refs["direct"]), near)
    own_real, own_imag = product(stacked(own_ref), 0)
    near_real, near_imag = product(near, 2 - odd)
    far_real, far_imag = product(far, 1 + odd)
    by_real = own_real + near_real + far_real
    by_imag = own_imag + near_imag + far_imag
    real = (by_real[:rows] - by_imag[rows:] + addend_ref[0].astype(jnp.float32)).astype(out_ref.dtype)
    imag = (by_imag[:rows] + by_real[rows:] + addend_ref[1].astype(jnp.float32)).astype(out_ref.dtype)
    out_ref[0] = real
    out_ref[1] = imag


def step(layer, kernel=step_kernel, **operands):
    vmem = pl.BlockSpec(memory_space=pltpu.VMEM)
    addend = operands["addend"]
    return pl.pallas_call(
        functools.partial(kernel, layer, tuple(operands)),
        out_shape=jax.ShapeDtypeStruct(addend.shape, addend.dtype),
        in_specs=[vmem] * len(operands),
        out_specs=vmem,
        compiler_params=pltpu.CompilerParams(vmem_limit_bytes=VMEM_LIMIT),
        cost_estimate=pl.CostEstimate(
            flops=24 * addend.shape[1] * addend.shape[2] * addend.shape[2],
            bytes_accessed=operands["blocks"].size * 2 + addend.size * 10,
            transcendentals=0,
        ),
    )(*operands.values())


def spread(values, source, target, order, near=near_mate, far=far_mate):
    tiles = lax.axis_size("tile")
    mates = {"far": far, "near": near, "own": same}
    return {name: permute(values, pairs_of(within_chip(source, target, mates[name]), tiles)) for name in order}


def hop(values, source, target, blocks, order, after=None, passed=None, **rest):
    if passed is None:
        arrived = spread(values, source, target, order)
    else:
        arrived = spread(values, source, target, order, far=inner_mate)
        rest = {"passed": passed, **rest}
    held = load(blocks, values if after is None else after, target)
    return step(target, **arrived, blocks=held, **rest)


def crossing_hop(values, source, target, blocks, order, addend):
    tiles = lax.axis_size("tile")
    relay = target ^ 1
    held = load(blocks, values, target)
    crossed = permute(values, across(source, target, tiles))
    seam = permute(values, else_on_chip(around(source, target, far_mate, far_mate), tiles, at_seam))
    direct = permute(values, else_on_chip(around(source, target, near_mate, over), tiles, by_seam))
    early = step(target, seam_kernel, far=seam, near=direct, own=crossed, blocks=held, addend=addend)
    passed = permute(early, else_on_chip(within_chip(target, relay, far_mate), tiles, at_seam))
    arrived = spread(crossed, relay, target, order, plain_mate, inner_mate)
    result = step(target, **arrived, direct=direct, early=early, blocks=held, addend=addend)
    return result, passed


def per_device(sources, down_blocks, up_blocks):
    layer = lax.axis_index("layer")
    source, down, up = sources[0], down_blocks[0], up_blocks[0]
    down_1 = hop(source, 0, 1, down, ORDERS[0], addend=source)
    down_2, passed = crossing_hop(down_1, 1, 2, down, ORDERS[1], addend=source)
    down_3 = hop(down_2, 2, 3, down, ORDERS[2], passed=passed, addend=source)
    falling = jnp.where(layer == 0, source, jnp.where(layer == 1, down_1, jnp.where(layer == 2, down_2, down_3)))
    up_2 = hop(down_3, 3, 2, up, ORDERS[3], addend=down_2)
    up_1, passed = crossing_hop(up_2, 2, 1, up, ORDERS[4], addend=down_1)
    rising = jnp.where(layer == 1, up_1, jnp.where(layer == 2, up_2, down_3))
    rising = hop(up_1, 1, 0, up, ORDERS[5], down_3, passed, addend=source, kept=rising)
    return (falling[None], rising[None])


def solution(mesh):
    return jax.shard_map(
        per_device,
        mesh=mesh,
        in_specs=(
            P("layer", None, None, "tile"),
            P("layer", None, None, "tile", None),
            P("layer", None, None, "tile", None),
        ),
        out_specs=(P("layer", None, None, "tile"), P("layer", None, None, "tile")),
        check_vma=False,
    )
```

```python
import functools

import jax
import jax.numpy as jnp
from jax import lax
from jax.experimental import pallas as pl
from jax.experimental.pallas import tpu as pltpu
from jax.sharding import PartitionSpec as P

AXES = ("layer", "tile")
VMEM_LIMIT = 16 * 1024 * 1024
FAR_FIRST = ("far", "near", "own")
ORDERS = (FAR_FIRST, FAR_FIRST, ("own", "far", "near"), FAR_FIRST, FAR_FIRST, FAR_FIRST)


def far_mate(tile, tiles):
    mate = tile + 1 if tile % 2 else tile - 1
    return mate if 0 <= mate < tiles else tile


def near_mate(tile, tiles):
    return tile - 1 if tile % 2 else tile + 1


def same(tile, tiles):
    return tile


def mirror(tile, tiles):
    x, z, y = tile // 16, tile // 4 % 4, tile % 4
    return 16 * x + 4 * (3 - z) + y


def at_seam(tile, tiles):
    return tile // 16 != far_mate(tile, tiles) // 16


def by_seam(tile, tiles):
    return at_seam(tile, tiles) or at_seam(near_mate(tile, tiles), tiles)


def inner_mate(tile, tiles):
    return tile if at_seam(tile, tiles) else far_mate(tile, tiles)


def plain_mate(tile, tiles):
    return tile if by_seam(tile, tiles) else near_mate(tile, tiles)


def over(tile, tiles):
    return (tile + 8) // 16 * 32 - 1 - tile


def pairs_of(route, tiles, select=lambda tile, tiles: True):
    return [
        (source * tiles + tile, target * tiles + mate(tile, tiles))
        for source, target, mate in route
        for tile in range(tiles)
        if select(tile, tiles)
    ]


ON_CHIP = ((0, 1, same), (1, 0, same), (2, 3, same), (3, 2, same))


def else_on_chip(route, tiles, select):
    return pairs_of(route, tiles, select) + pairs_of(ON_CHIP, tiles, lambda *tile: not select(*tile))


def within_chip(source, target, mate):
    one, two = [layer for layer in range(4) if layer not in (source, target)]
    return ((source, target, mate), (target, source, same), (one, two, same), (two, one, same))


def around(source, target, mate, back):
    return (
        (source, target, mate),
        (target, target ^ 1, same),
        (target ^ 1, source ^ 1, back),
        (source ^ 1, source, same),
    )


def across(source, target, tiles):
    return pairs_of(around(source, target, same, mirror), tiles, at_seam) + pairs_of(
        around(source, target ^ 1, same, mirror), tiles, lambda *tile: not at_seam(*tile)
    )


def permute(values, pairs):
    return lax.ppermute(values, AXES, pairs)


def load_kernel(layers, blocks_ref, after_ref, held_ref, sems):
    here = lax.axis_index("layer")

    @pl.when(functools.reduce(jnp.logical_or, [here == layer for layer in layers]))
    def _():
        count, parts = blocks_ref.shape[:2]
        copies = [
            pltpu.make_async_copy(blocks_ref.at[i, j], held_ref.at[i, j], sems.at[i, j])
            for i in range(count)
            for j in range(parts)
        ]
        for copy in copies:
            copy.start()
        for copy in copies:
            copy.wait()


def load(blocks, after, *layers):
    return pl.pallas_call(
        functools.partial(load_kernel, layers),
        out_shape=pltpu.VMEM(blocks.shape, blocks.dtype),
        in_specs=[pl.BlockSpec(memory_space=pl.ANY)] * 2,
        out_specs=pl.BlockSpec(memory_space=pltpu.VMEM),
        scratch_shapes=[pltpu.SemaphoreType.DMA(blocks.shape[:2])],
        compiler_params=pltpu.CompilerParams(vmem_limit_bytes=VMEM_LIMIT),
        cost_estimate=pl.CostEstimate(flops=0, bytes_accessed=blocks.size * 4, transcendentals=0),
    )(pltpu.with_memory_space_constraint(blocks, pltpu.HBM), after)


def seam_here(shift):
    tiles = lax.axis_size("tile")
    tile = lax.axis_index("tile")
    run = tiles // 4
    place = lax.rem(tile, run)
    outer = jnp.logical_or(tile == shift, tile == tiles - 1 - shift)
    return jnp.logical_and(jnp.logical_or(place == shift, place == run - 1 - shift), jnp.logical_not(outer))


def step_kernel(layer, names, *refs):
    *refs, out_ref = refs
    refs = dict(zip(names, refs))
    here = lax.axis_index("layer") == layer
    if "early" in refs:
        seam = seam_here(0)

        @pl.when(jnp.logical_and(here, seam))
        def _():
            out_ref[...] = refs["early"][...]

        here = jnp.logical_and(here, jnp.logical_not(seam))

    if "kept" in refs:

        @pl.when(jnp.logical_not(here))
        def _():
            out_ref[...] = refs["kept"][...]

    @pl.when(here)
    def _():
        product_and_sum(refs, out_ref)


def seam_kernel(layer, names, *refs):
    *refs, out_ref = refs

    @pl.when(jnp.logical_and(lax.axis_index("layer") == layer, seam_here(0)))
    def _():
        product_and_sum(dict(zip(names, refs)), out_ref)


def product_and_sum(refs, out_ref):
    own_ref, near_ref, far_ref = refs["own"], refs["near"], refs["far"]
    blocks_ref, addend_ref = refs["blocks"], refs["addend"]
    tiles = lax.axis_size("tile")
    tile = lax.axis_index("tile")
    odd = lax.rem(tile, 2)
    rows, cells = own_ref.shape[1:]
    edge = jnp.logical_or(tile == 0, tile == tiles - 1)

    def stacked(ref):
        return ref[...].reshape(2 * rows, cells)

    def product(values, number):
        by_real = jnp.dot(values, blocks_ref[number, 0], preferred_element_type=jnp.float32)
        by_imag = jnp.dot(values, blocks_ref[number, 1], preferred_element_type=jnp.float32)
        return by_real, by_imag

    far = stacked(far_ref)
    if "passed" in refs:
        far = jnp.where(seam_here(0), stacked(refs["passed"]), far)
    far = jnp.where(edge, jnp.zeros_like(far), far)
    near = stacked(near_ref)
    if "direct" in refs:
        near = jnp.where(seam_here(1), stacked(refs["direct"]), near)
    own_real, own_imag = product(stacked(own_ref), 0)
    near_real, near_imag = product(near, 2 - odd)
    far_real, far_imag = product(far, 1 + odd)
    by_real = own_real + near_real + far_real
    by_imag = own_imag + near_imag + far_imag
    real = (by_real[:rows] - by_imag[rows:] + addend_ref[0].astype(jnp.float32)).astype(out_ref.dtype)
    imag = (by_imag[:rows] + by_real[rows:] + addend_ref[1].astype(jnp.float32)).astype(out_ref.dtype)
    out_ref[0] = real
    out_ref[1] = imag


def step(layer, kernel=step_kernel, **operands):
    vmem = pl.BlockSpec(memory_space=pltpu.VMEM)
    addend = operands["addend"]
    return pl.pallas_call(
        functools.partial(kernel, layer, tuple(operands)),
        out_shape=jax.ShapeDtypeStruct(addend.shape, addend.dtype),
        in_specs=[vmem] * len(operands),
        out_specs=vmem,
        compiler_params=pltpu.CompilerParams(vmem_limit_bytes=VMEM_LIMIT),
        cost_estimate=pl.CostEstimate(
            flops=24 * addend.shape[1] * addend.shape[2] * addend.shape[2],
            bytes_accessed=operands["blocks"].size * 2 + addend.size * 10,
            transcendentals=0,
        ),
    )(*operands.values())


def spread(values, source, target, order, near=near_mate, far=far_mate):
    tiles = lax.axis_size("tile")
    mates = {"far": far, "near": near, "own": same}
    return {name: permute(values, pairs_of(within_chip(source, target, mates[name]), tiles)) for name in order}


def hop(values, source, target, blocks, order, after=None, passed=None, **rest):
    if passed is None:
        arrived = spread(values, source, target, order)
    else:
        arrived = spread(values, source, target, order, far=inner_mate)
        rest = {"passed": passed, **rest}
    held = load(blocks, values if after is None else after, target)
    return step(target, **arrived, blocks=held, **rest)


def crossing_hop(values, source, target, blocks, order, addend):
    tiles = lax.axis_size("tile")
    relay = target ^ 1
    held = load(blocks, values, target)
    crossed = permute(values, across(source, target, tiles))
    seam = permute(values, else_on_chip(around(source, target, far_mate, far_mate), tiles, at_seam))
    direct = permute(values, else_on_chip(around(source, target, near_mate, over), tiles, by_seam))
    early = step(target, seam_kernel, far=seam, near=direct, own=crossed, blocks=held, addend=addend)
    passed = permute(early, else_on_chip(within_chip(target, relay, far_mate), tiles, at_seam))
    arrived = spread(crossed, relay, target, order, plain_mate, inner_mate)
    result = step(target, **arrived, direct=direct, early=early, blocks=held, addend=addend)
    return result, passed


def per_device(sources, down_blocks, up_blocks):
    layer = lax.axis_index("layer")
    source, down, up = sources[0], down_blocks[0], up_blocks[0]
    down_1 = hop(source, 0, 1, down, ORDERS[0], addend=source)
    down_2, passed = crossing_hop(down_1, 1, 2, down, ORDERS[1], addend=source)
    down_3 = hop(down_2, 2, 3, down, ORDERS[2], passed=passed, addend=source)
    falling = jnp.where(layer == 0, source, jnp.where(layer == 1, down_1, jnp.where(layer == 2, down_2, down_3)))
    up_2 = hop(down_3, 3, 2, up, ORDERS[3], addend=down_2)
    up_1, passed = crossing_hop(up_2, 2, 1, up, ORDERS[4], addend=down_1)
    rising = jnp.where(layer == 1, up_1, jnp.where(layer == 2, up_2, down_3))
    rising = hop(up_1, 1, 0, up, ORDERS[5], rising, passed, addend=source, kept=rising)
    return (falling[None], rising[None])


def solution(mesh):
    return jax.shard_map(
        per_device,
        mesh=mesh,
        in_specs=(
            P("layer", None, None, "tile"),
            P("layer", None, None, "tile", None),
            P("layer", None, None, "tile", None),
        ),
        out_specs=(P("layer", None, None, "tile"), P("layer", None, None, "tile")),
        check_vma=False,
    )
```

```python
import functools

import jax
import jax.numpy as jnp
from jax import lax
from jax.experimental import pallas as pl
from jax.experimental.pallas import tpu as pltpu
from jax.sharding import PartitionSpec as P

AXES = ("layer", "tile")
VMEM_LIMIT = 16 * 1024 * 1024
FAR_FIRST = ("far", "near", "own")
ORDERS = (FAR_FIRST, FAR_FIRST, ("own", "far", "near"), FAR_FIRST, FAR_FIRST, FAR_FIRST)


def far_mate(tile, tiles):
    mate = tile + 1 if tile % 2 else tile - 1
    return mate if 0 <= mate < tiles else tile


def near_mate(tile, tiles):
    return tile - 1 if tile % 2 else tile + 1


def same(tile, tiles):
    return tile


def mirror(tile, tiles):
    x, z, y = tile // 16, tile // 4 % 4, tile % 4
    return 16 * x + 4 * (3 - z) + y


def at_seam(tile, tiles):
    return tile // 16 != far_mate(tile, tiles) // 16


def by_seam(tile, tiles):
    return at_seam(tile, tiles) or at_seam(near_mate(tile, tiles), tiles)


def inner_mate(tile, tiles):
    return tile if at_seam(tile, tiles) else far_mate(tile, tiles)


def plain_mate(tile, tiles):
    return tile if by_seam(tile, tiles) else near_mate(tile, tiles)


def over(tile, tiles):
    return (tile + 8) // 16 * 32 - 1 - tile


def pairs_of(route, tiles, select=lambda tile, tiles: True):
    return [
        (source * tiles + tile, target * tiles + mate(tile, tiles))
        for source, target, mate in route
        for tile in range(tiles)
        if select(tile, tiles)
    ]


ON_CHIP = ((0, 1, same), (1, 0, same), (2, 3, same), (3, 2, same))


def else_on_chip(route, tiles, select):
    return pairs_of(route, tiles, select) + pairs_of(ON_CHIP, tiles, lambda *tile: not select(*tile))


def within_chip(source, target, mate):
    one, two = [layer for layer in range(4) if layer not in (source, target)]
    return ((source, target, mate), (target, source, same), (one, two, same), (two, one, same))


def around(source, target, mate, back):
    return (
        (source, target, mate),
        (target, target ^ 1, same),
        (target ^ 1, source ^ 1, back),
        (source ^ 1, source, same),
    )


def across(source, target, tiles):
    return pairs_of(around(source, target, same, mirror), tiles, at_seam) + pairs_of(
        around(source, target ^ 1, same, mirror), tiles, lambda *tile: not at_seam(*tile)
    )


def permute(values, pairs):
    return lax.ppermute(values, AXES, pairs)


def load_kernel(layers, blocks_ref, after_ref, held_ref, sems):
    here = lax.axis_index("layer")

    @pl.when(functools.reduce(jnp.logical_or, [here == layer for layer in layers]))
    def _():
        count, parts = blocks_ref.shape[:2]
        copies = [
            pltpu.make_async_copy(blocks_ref.at[i, j], held_ref.at[i, j], sems.at[i, j])
            for i in range(count)
            for j in range(parts)
        ]
        for copy in copies:
            copy.start()
        for copy in copies:
            copy.wait()


def load(blocks, after, *layers):
    return pl.pallas_call(
        functools.partial(load_kernel, layers),
        out_shape=pltpu.VMEM(blocks.shape, blocks.dtype),
        in_specs=[pl.BlockSpec(memory_space=pl.ANY)] * 2,
        out_specs=pl.BlockSpec(memory_space=pltpu.VMEM),
        scratch_shapes=[pltpu.SemaphoreType.DMA(blocks.shape[:2])],
        compiler_params=pltpu.CompilerParams(vmem_limit_bytes=VMEM_LIMIT),
        cost_estimate=pl.CostEstimate(flops=0, bytes_accessed=blocks.size * 4, transcendentals=0),
    )(pltpu.with_memory_space_constraint(blocks, pltpu.HBM), after)


def seam_here(shift):
    tiles = lax.axis_size("tile")
    tile = lax.axis_index("tile")
    run = tiles // 4
    place = lax.rem(tile, run)
    outer = jnp.logical_or(tile == shift, tile == tiles - 1 - shift)
    return jnp.logical_and(jnp.logical_or(place == shift, place == run - 1 - shift), jnp.logical_not(outer))


def step_kernel(layer, names, *refs):
    *refs, out_ref = refs
    refs = dict(zip(names, refs))
    here = lax.axis_index("layer") == layer
    if "early" in refs:
        seam = seam_here(0)

        @pl.when(jnp.logical_and(here, seam))
        def _():
            out_ref[...] = refs["early"][...]

        here = jnp.logical_and(here, jnp.logical_not(seam))

    if "kept" in refs:

        @pl.when(jnp.logical_not(here))
        def _():
            out_ref[...] = refs["kept"][...]

    @pl.when(here)
    def _():
        product_and_sum(refs, out_ref)


def seam_kernel(layer, names, *refs):
    *refs, out_ref = refs

    @pl.when(jnp.logical_and(lax.axis_index("layer") == layer, seam_here(0)))
    def _():
        product_and_sum(dict(zip(names, refs)), out_ref)


def product_and_sum(refs, out_ref):
    own_ref, near_ref, far_ref = refs["own"], refs["near"], refs["far"]
    blocks_ref, addend_ref = refs["blocks"], refs["addend"]
    tiles = lax.axis_size("tile")
    tile = lax.axis_index("tile")
    odd = lax.rem(tile, 2)
    rows, cells = own_ref.shape[1:]
    edge = jnp.logical_or(tile == 0, tile == tiles - 1)

    def stacked(ref):
        return ref[...].reshape(2 * rows, cells)

    def product(values, number):
        by_real = jnp.dot(values, blocks_ref[number, 0], preferred_element_type=jnp.float32)
        by_imag = jnp.dot(values, blocks_ref[number, 1], preferred_element_type=jnp.float32)
        return by_real, by_imag

    far = stacked(far_ref)
    if "passed" in refs:
        far = jnp.where(seam_here(0), stacked(refs["passed"]), far)
    far = jnp.where(edge, jnp.zeros_like(far), far)
    near = stacked(near_ref)
    if "direct" in refs:
        near = jnp.where(seam_here(1), stacked(refs["direct"]), near)
    own_real, own_imag = product(stacked(own_ref), 0)
    near_real, near_imag = product(near, 2 - odd)
    far_real, far_imag = product(far, 1 + odd)
    by_real = own_real + near_real + far_real
    by_imag = own_imag + near_imag + far_imag
    real = (by_real[:rows] - by_imag[rows:] + addend_ref[0].astype(jnp.float32)).astype(out_ref.dtype)
    imag = (by_imag[:rows] + by_real[rows:] + addend_ref[1].astype(jnp.float32)).astype(out_ref.dtype)
    out_ref[0] = real
    out_ref[1] = imag


def step(layer, kernel=step_kernel, **operands):
    vmem = pl.BlockSpec(memory_space=pltpu.VMEM)
    addend = operands["addend"]
    return pl.pallas_call(
        functools.partial(kernel, layer, tuple(operands)),
        out_shape=jax.ShapeDtypeStruct(addend.shape, addend.dtype),
        in_specs=[vmem] * len(operands),
        out_specs=vmem,
        compiler_params=pltpu.CompilerParams(vmem_limit_bytes=VMEM_LIMIT),
        cost_estimate=pl.CostEstimate(
            flops=24 * addend.shape[1] * addend.shape[2] * addend.shape[2],
            bytes_accessed=operands["blocks"].size * 2 + addend.size * 10,
            transcendentals=0,
        ),
    )(*operands.values())


def spread(values, source, target, order, near=near_mate, far=far_mate):
    tiles = lax.axis_size("tile")
    mates = {"far": far, "near": near, "own": same}
    return {name: permute(values, pairs_of(within_chip(source, target, mates[name]), tiles)) for name in order}


def hop(values, source, target, blocks, order, after=None, passed=None, **rest):
    if passed is None:
        arrived = spread(values, source, target, order)
    else:
        arrived = spread(values, source, target, order, far=inner_mate)
        rest = {"passed": passed, **rest}
    held = load(blocks, values if after is None else after, target)
    return step(target, **arrived, blocks=held, **rest)


def crossing_hop(values, source, target, blocks, order, addend):
    tiles = lax.axis_size("tile")
    relay = target ^ 1
    held = load(blocks, values, target)
    crossed = permute(values, across(source, target, tiles))
    seam = permute(values, else_on_chip(around(source, target, far_mate, same), tiles, at_seam))
    direct = permute(values, else_on_chip(around(source, target, near_mate, over), tiles, by_seam))
    early = step(target, seam_kernel, far=seam, near=direct, own=crossed, blocks=held, addend=addend)
    passed = permute(early, else_on_chip(within_chip(target, relay, far_mate), tiles, at_seam))
    arrived = spread(crossed, relay, target, order, plain_mate, inner_mate)
    result = step(target, **arrived, direct=direct, early=early, blocks=held, addend=addend)
    return result, passed


def per_device(sources, down_blocks, up_blocks):
    layer = lax.axis_index("layer")
    source, down, up = sources[0], down_blocks[0], up_blocks[0]
    down_1 = hop(source, 0, 1, down, ORDERS[0], addend=source)
    down_2, passed = crossing_hop(down_1, 1, 2, down, ORDERS[1], addend=source)
    down_3 = hop(down_2, 2, 3, down, ORDERS[2], passed=passed, addend=source)
    falling = jnp.where(layer == 0, source, jnp.where(layer == 1, down_1, jnp.where(layer == 2, down_2, down_3)))
    up_2 = hop(down_3, 3, 2, up, ORDERS[3], addend=down_2)
    up_1, passed = crossing_hop(up_2, 2, 1, up, ORDERS[4], addend=down_1)
    rising = jnp.where(layer == 1, up_1, jnp.where(layer == 2, up_2, down_3))
    rising = hop(up_1, 1, 0, up, ORDERS[5], rising, passed, addend=source, kept=rising)
    return (falling[None], rising[None])


def solution(mesh):
    return jax.shard_map(
        per_device,
        mesh=mesh,
        in_specs=(
            P("layer", None, None, "tile"),
            P("layer", None, None, "tile", None),
            P("layer", None, None, "tile", None),
        ),
        out_specs=(P("layer", None, None, "tile"), P("layer", None, None, "tile")),
        check_vma=False,
    )
```

```python
import functools

import jax
import jax.numpy as jnp
from jax import lax
from jax.experimental import pallas as pl
from jax.experimental.pallas import tpu as pltpu
from jax.sharding import PartitionSpec as P

AXES = ("layer", "tile")
VMEM_LIMIT = 16 * 1024 * 1024
FAR_FIRST = ("far", "near", "own")
ORDERS = (FAR_FIRST, FAR_FIRST, ("own", "far", "near"), FAR_FIRST, FAR_FIRST, FAR_FIRST)


def far_mate(tile, tiles):
    mate = tile + 1 if tile % 2 else tile - 1
    return mate if 0 <= mate < tiles else tile


def near_mate(tile, tiles):
    return tile - 1 if tile % 2 else tile + 1


def same(tile, tiles):
    return tile


def mirror(tile, tiles):
    x, z, y = tile // 16, tile // 4 % 4, tile % 4
    return 16 * x + 4 * (3 - z) + y


def at_seam(tile, tiles):
    return tile // 16 != far_mate(tile, tiles) // 16


def by_seam(tile, tiles):
    return at_seam(tile, tiles) or at_seam(near_mate(tile, tiles), tiles)


def inner_mate(tile, tiles):
    return tile if at_seam(tile, tiles) else far_mate(tile, tiles)


def plain_mate(tile, tiles):
    return tile if by_seam(tile, tiles) else near_mate(tile, tiles)


def over(tile, tiles):
    return (tile + 8) // 16 * 32 - 1 - tile


def pairs_of(route, tiles, select=lambda tile, tiles: True):
    return [
        (source * tiles + tile, target * tiles + mate(tile, tiles))
        for source, target, mate in route
        for tile in range(tiles)
        if select(tile, tiles)
    ]


ON_CHIP = ((0, 1, same), (1, 0, same), (2, 3, same), (3, 2, same))


def else_on_chip(route, tiles, select):
    return pairs_of(route, tiles, select) + pairs_of(ON_CHIP, tiles, lambda *tile: not select(*tile))


def within_chip(source, target, mate):
    one, two = [layer for layer in range(4) if layer not in (source, target)]
    return ((source, target, mate), (target, source, same), (one, two, same), (two, one, same))


def around(source, target, mate, back):
    return (
        (source, target, mate),
        (target, target ^ 1, same),
        (target ^ 1, source ^ 1, back),
        (source ^ 1, source, same),
    )


def across(source, target, tiles):
    return pairs_of(around(source, target, same, mirror), tiles, at_seam) + pairs_of(
        around(source, target ^ 1, same, mirror), tiles, lambda *tile: not at_seam(*tile)
    )


def permute(values, pairs):
    return lax.ppermute(values, AXES, pairs)


def load_kernel(layers, blocks_ref, after_ref, held_ref, sems):
    here = lax.axis_index("layer")

    @pl.when(functools.reduce(jnp.logical_or, [here == layer for layer in layers]))
    def _():
        count, parts = blocks_ref.shape[:2]
        copies = [
            pltpu.make_async_copy(blocks_ref.at[i, j], held_ref.at[i, j], sems.at[i, j])
            for i in range(count)
            for j in range(parts)
        ]
        for copy in copies:
            copy.start()
        for copy in copies:
            copy.wait()


def load(blocks, after, *layers):
    return pl.pallas_call(
        functools.partial(load_kernel, layers),
        out_shape=pltpu.VMEM(blocks.shape, blocks.dtype),
        in_specs=[pl.BlockSpec(memory_space=pl.ANY)] * 2,
        out_specs=pl.BlockSpec(memory_space=pltpu.VMEM),
        scratch_shapes=[pltpu.SemaphoreType.DMA(blocks.shape[:2])],
        compiler_params=pltpu.CompilerParams(vmem_limit_bytes=VMEM_LIMIT),
        cost_estimate=pl.CostEstimate(flops=0, bytes_accessed=blocks.size * 4, transcendentals=0),
    )(pltpu.with_memory_space_constraint(blocks, pltpu.HBM), after)


def seam_here(shift):
    tiles = lax.axis_size("tile")
    tile = lax.axis_index("tile")
    run = tiles // 4
    place = lax.rem(tile, run)
    outer = jnp.logical_or(tile == shift, tile == tiles - 1 - shift)
    return jnp.logical_and(jnp.logical_or(place == shift, place == run - 1 - shift), jnp.logical_not(outer))


def step_kernel(layer, names, *refs):
    *refs, out_ref = refs
    refs = dict(zip(names, refs))
    here = lax.axis_index("layer") == layer
    if "early" in refs:
        seam = seam_here(0)

        @pl.when(jnp.logical_and(here, seam))
        def _():
            out_ref[...] = refs["early"][...]

        here = jnp.logical_and(here, jnp.logical_not(seam))

    if "kept" in refs:

        @pl.when(jnp.logical_not(here))
        def _():
            out_ref[...] = refs["kept"][...]

    @pl.when(here)
    def _():
        product_and_sum(refs, out_ref)


def seam_kernel(layer, names, *refs):
    *refs, out_ref = refs

    @pl.when(jnp.logical_and(lax.axis_index("layer") == layer, seam_here(0)))
    def _():
        product_and_sum(dict(zip(names, refs)), out_ref)


def product_and_sum(refs, out_ref):
    own_ref, near_ref, far_ref = refs["own"], refs["near"], refs["far"]
    blocks_ref, addend_ref = refs["blocks"], refs["addend"]
    tiles = lax.axis_size("tile")
    tile = lax.axis_index("tile")
    odd = lax.rem(tile, 2)
    rows, cells = own_ref.shape[1:]
    edge = jnp.logical_or(tile == 0, tile == tiles - 1)

    def stacked(ref):
        return ref[...].reshape(2 * rows, cells)

    def product(values, number):
        by_real = jnp.dot(values, blocks_ref[number, 0], preferred_element_type=jnp.float32)
        by_imag = jnp.dot(values, blocks_ref[number, 1], preferred_element_type=jnp.float32)
        return by_real, by_imag

    far = stacked(far_ref)
    if "passed" in refs:
        far = jnp.where(seam_here(0), stacked(refs["passed"]), far)
    far = jnp.where(edge, jnp.zeros_like(far), far)
    near = stacked(near_ref)
    if "direct" in refs:
        near = jnp.where(seam_here(1), stacked(refs["direct"]), near)
    own_real, own_imag = product(stacked(own_ref), 0)
    near_real, near_imag = product(near, 2 - odd)
    far_real, far_imag = product(far, 1 + odd)
    by_real = own_real + near_real + far_real
    by_imag = own_imag + near_imag + far_imag
    real = (by_real[:rows] - by_imag[rows:] + addend_ref[0].astype(jnp.float32)).astype(out_ref.dtype)
    imag = (by_imag[:rows] + by_real[rows:] + addend_ref[1].astype(jnp.float32)).astype(out_ref.dtype)
    out_ref[0] = real
    out_ref[1] = imag


def first_kernel(layer, names, *refs):
    *refs, sum_ref = refs
    refs = dict(zip(names, refs))

    @pl.when(lax.axis_index("layer") == layer)
    def _():
        rows = refs["own"].shape[1]
        near_number = 2 - lax.rem(lax.axis_index("tile"), 2)
        by_real = jnp.zeros(sum_ref.shape[1:], jnp.float32)
        by_imag = by_real
        for name, number in (("own", 0), ("near", near_number)):
            values = refs[name][...].reshape(2 * rows, -1)
            by_real += jnp.dot(values, refs["blocks"][number, 0], preferred_element_type=jnp.float32)
            by_imag += jnp.dot(values, refs["blocks"][number, 1], preferred_element_type=jnp.float32)
        sum_ref[0] = by_real
        sum_ref[1] = by_imag


def last_kernel(layer, names, *refs):
    *refs, out_ref = refs
    refs = dict(zip(names, refs))
    here = lax.axis_index("layer") == layer

    @pl.when(jnp.logical_not(here))
    def _():
        out_ref[...] = refs["kept"][...]

    @pl.when(here)
    def _():
        tile = lax.axis_index("tile")
        rows, cells = refs["far"].shape[1:]
        edge = jnp.logical_or(tile == 0, tile == lax.axis_size("tile") - 1)
        far = jnp.where(seam_here(0), refs["passed"][...], refs["far"][...]).reshape(2 * rows, cells)
        far = jnp.where(edge, jnp.zeros_like(far), far)
        number = 1 + lax.rem(tile, 2)
        by_real = refs["sums"][0] + jnp.dot(far, refs["blocks"][number, 0], preferred_element_type=jnp.float32)
        by_imag = refs["sums"][1] + jnp.dot(far, refs["blocks"][number, 1], preferred_element_type=jnp.float32)
        addend_ref = refs["addend"]
        out_ref[0] = (by_real[:rows] - by_imag[rows:] + addend_ref[0].astype(jnp.float32)).astype(out_ref.dtype)
        out_ref[1] = (by_imag[:rows] + by_real[rows:] + addend_ref[1].astype(jnp.float32)).astype(out_ref.dtype)


def call(kernel, layer, shape, dtype, flops, **operands):
    vmem = pl.BlockSpec(memory_space=pltpu.VMEM)
    return pl.pallas_call(
        functools.partial(kernel, layer, tuple(operands)),
        out_shape=jax.ShapeDtypeStruct(shape, dtype),
        in_specs=[vmem] * len(operands),
        out_specs=vmem,
        compiler_params=pltpu.CompilerParams(vmem_limit_bytes=VMEM_LIMIT),
        cost_estimate=pl.CostEstimate(flops=flops, bytes_accessed=operands["blocks"].size, transcendentals=0),
    )(*operands.values())


def last_hop(values, source, target, held, order, passed, addend, kept):
    arrived = spread(values, source, target, order, far=inner_mate)
    parts, rows, cells = addend.shape
    flops = 8 * rows * cells * cells
    sums = call(first_kernel, target, (2, parts * rows, cells), jnp.float32, 2 * flops, near=arrived["near"], own=arrived["own"], blocks=held)
    return call(last_kernel, target, addend.shape, addend.dtype, flops, far=arrived["far"], passed=passed, sums=sums, blocks=held, addend=addend, kept=kept)


def step(layer, kernel=step_kernel, **operands):
    vmem = pl.BlockSpec(memory_space=pltpu.VMEM)
    addend = operands["addend"]
    return pl.pallas_call(
        functools.partial(kernel, layer, tuple(operands)),
        out_shape=jax.ShapeDtypeStruct(addend.shape, addend.dtype),
        in_specs=[vmem] * len(operands),
        out_specs=vmem,
        compiler_params=pltpu.CompilerParams(vmem_limit_bytes=VMEM_LIMIT),
        cost_estimate=pl.CostEstimate(
            flops=24 * addend.shape[1] * addend.shape[2] * addend.shape[2],
            bytes_accessed=operands["blocks"].size * 2 + addend.size * 10,
            transcendentals=0,
        ),
    )(*operands.values())


def spread(values, source, target, order, near=near_mate, far=far_mate):
    tiles = lax.axis_size("tile")
    mates = {"far": far, "near": near, "own": same}
    return {name: permute(values, pairs_of(within_chip(source, target, mates[name]), tiles)) for name in order}


def hop(values, source, target, blocks, order, after=None, passed=None, **rest):
    if passed is None:
        arrived = spread(values, source, target, order)
    else:
        arrived = spread(values, source, target, order, far=inner_mate)
        rest = {"passed": passed, **rest}
    held = load(blocks, values if after is None else after, target)
    return step(target, **arrived, blocks=held, **rest)


def crossing_hop(values, source, target, blocks, order, addend):
    tiles = lax.axis_size("tile")
    relay = target ^ 1
    held = load(blocks, values, target)
    crossed = permute(values, across(source, target, tiles))
    seam = permute(values, else_on_chip(around(source, target, far_mate, same), tiles, at_seam))
    direct = permute(values, else_on_chip(around(source, target, near_mate, over), tiles, by_seam))
    early = step(target, seam_kernel, far=seam, near=direct, own=crossed, blocks=held, addend=addend)
    passed = permute(early, else_on_chip(within_chip(target, relay, far_mate), tiles, at_seam))
    arrived = spread(crossed, relay, target, order, plain_mate, inner_mate)
    result = step(target, **arrived, direct=direct, early=early, blocks=held, addend=addend)
    return result, passed


def per_device(sources, down_blocks, up_blocks):
    layer = lax.axis_index("layer")
    source, down, up = sources[0], down_blocks[0], up_blocks[0]
    down_1 = hop(source, 0, 1, down, ORDERS[0], addend=source)
    down_2, passed = crossing_hop(down_1, 1, 2, down, ORDERS[1], addend=source)
    down_3 = hop(down_2, 2, 3, down, ORDERS[2], passed=passed, addend=source)
    falling = jnp.where(layer == 0, source, jnp.where(layer == 1, down_1, jnp.where(layer == 2, down_2, down_3)))
    up_2 = hop(down_3, 3, 2, up, ORDERS[3], addend=down_2)
    up_1, passed = crossing_hop(up_2, 2, 1, up, ORDERS[4], addend=down_1)
    rising = jnp.where(layer == 1, up_1, jnp.where(layer == 2, up_2, down_3))
    rising = last_hop(up_1, 1, 0, load(up, rising, 0), ORDERS[5], passed, source, rising)
    return (falling[None], rising[None])


def solution(mesh):
    return jax.shard_map(
        per_device,
        mesh=mesh,
        in_specs=(
            P("layer", None, None, "tile"),
            P("layer", None, None, "tile", None),
            P("layer", None, None, "tile", None),
        ),
        out_specs=(P("layer", None, None, "tile"), P("layer", None, None, "tile")),
        check_vma=False,
    )
```
